32 devices in a mesh: groups: 2 (over x), ctx: 16 (over z, y, core).
Axes of the slice: x: 2, y: 2, z: 4, core: 2. Of those that a mesh axis runs over, the one named last changes fastest.
Arguments:
- projected: bfloat16 [4096, 6144], P(('groups', 'ctx')), parts along dimension 0, may hold values from -6 to 6
- short_filter: float32 [3, 6144], replicated, may hold values from -3.5 to 3.5
- modal_pole: float32 [2048, 16], replicated, may hold values from 0.96 to 1, as said below
- residue: float32 [2048, 16], replicated, may hold values from -1.5 to 1.5
- skip_weight: float32 [2048], replicated, may hold values from -3 to 3
- out_weight: bfloat16 [2048, 4096], P('ctx'), may hold values from -0.125 to 0.125
Outputs:
- block_output: bfloat16 [4096, 4096], P(('groups', 'ctx')), parts along dimension 0
The draws below stay inside these ranges and needn't reach their ends.
There are 2 independent parts, one for each index of `groups`. The reference program is written for one: setup_inputs(seed, part) draws one part's arguments, and reference() takes and returns one part's arrays. A program takes and returns all parts, laid end to end along the dimension named above; an argument that names none is the same for every part. Nothing has to cross between parts.
Inputs may be any that keep to these rules, and one draw needn't show every extreme that they name: `modal_pole`: every pole lies strictly between 0 and 1.
All inputs are finite; a program needn't handle non-finite values.
Results may differ from the reference program's by a relative error of at most 0.005.
Values may be sent and summed in bfloat16 or wider, within the bound.
A program may use at most 128 MiB of HBM per device.

```python
import jax
import jax.numpy as jnp
from jax import lax

WIDTH = 4096
POLES = 16
CHANNELS = 2048
TOKENS = 2048


def draw_modal_pole(key, part):
    low_rate = 0.01 / TOKENS
    high_rate = 1.0 / 30.0
    fraction = jax.random.uniform(key, (CHANNELS, POLES), jnp.float32)
    log_low = jnp.log(jnp.float32(low_rate))
    log_high = jnp.log(jnp.float32(high_rate))
    rate_value = jnp.exp(log_low + fraction * (log_high - log_low))
    return jnp.exp(-rate_value)


def block_scale(stream_key, shape, pieces, smallest, high):
    gain = 1.0
    for dim, parts in pieces:
        steps = jax.random.uniform(jax.random.fold_in(jax.random.fold_in(stream_key, 6), dim), (parts,), jnp.float32, smallest / len(pieces), high / len(pieces))
        gain = gain * jnp.repeat(jnp.exp(steps), shape[dim] // parts).reshape((-1,) + (1,) * (len(shape) - 1 - dim))
    return gain


def bell_draw(stream_key, extent, width, limit, split=(), dtype=jnp.bfloat16):
    gain = block_scale(stream_key, extent, split, -0.22, 0.18) if split else 1.0
    drawn = jax.random.normal(stream_key, extent, jnp.float32) * width * gain
    return jnp.minimum(jnp.maximum(drawn, -limit), limit).astype(dtype)


def setup_inputs(seed: int = 0, part: int = 0) -> dict:
    keys = jax.random.split(jax.random.key(seed), 7)
    part_splits = jax.random.split(jax.random.fold_in(keys[6], part), 7)
    return {
        "projected": bell_draw(part_splits[0], (TOKENS, 3 * CHANNELS), 1.0, 6.0, ((0, 16),)),
        "short_filter": bell_draw(keys[1], (3, 3 * CHANNELS), 3 ** -0.5, 3.5, (), jnp.float32),
        "modal_pole": draw_modal_pole(jax.random.fold_in(keys[6], 71), part),
        "residue": bell_draw(keys[3], (CHANNELS, POLES), 0.25, 1.5, (), jnp.float32),
        "skip_weight": bell_draw(keys[4], (CHANNELS,), 0.5, 3.0, (), jnp.float32),
        "out_weight": bell_draw(keys[5], (CHANNELS, WIDTH), CHANNELS ** -0.5, 0.125, ((0, 16),)),
    }


def reference(projected, short_filter, modal_pole, residue, skip_weight, out_weight):
    chan_count = modal_pole.shape[0]
    inputs = projected.astype(jnp.float32)
    extended = jnp.concatenate([jnp.zeros((2, inputs.shape[1]), jnp.float32), inputs], 0)
    smoothed = short_filter[0] * extended[2:] + short_filter[1] * extended[1:-1] + short_filter[2] * extended[:-2]
    query_part = smoothed[:, :chan_count]
    drive = smoothed[:, chan_count:2 * chan_count] * smoothed[:, 2 * chan_count:]
    input_gain = jnp.sqrt((1.0 - modal_pole) * (1.0 + modal_pole))

    def token_step(modal_state, drive_now):
        modal_state = modal_pole * modal_state + input_gain * drive_now[:, None]
        return (modal_state, lax.optimization_barrier(jnp.sum(residue * modal_state, 1)))
    _, filtered = lax.scan(token_step, jnp.zeros(modal_pole.shape, jnp.float32), drive)
    filtered = filtered + skip_weight * drive
    gated_rows = (query_part * filtered).astype(jnp.bfloat16)
    return jnp.dot(gated_rows, out_weight, preferred_element_type=jnp.float32).astype(jnp.bfloat16)
```

```python
import functools

import jax
import jax.numpy as jnp
from jax import lax
from jax.experimental import pallas as pl
from jax.experimental.pallas import tpu as pltpu
from jax.sharding import PartitionSpec as P

MESH = pl.DeviceIdType.MESH
LANES = 128
PHASES = 4
SKEW = 3


def kernel(
    ctx_count, proj, taps, pole, res, skip, w_in, out,
    halo, pole_t, coef_t, decay, drive, filt, query, sent, came, gated, w_all, prod,
    halo_sem, mate_sem, own_sem, ring_send, ring_recv, state_sem, gate_sem, fwd_sem, prod_sem, keep_sem,
):
    group = lax.axis_index("groups")
    ctx = lax.axis_index("ctx")
    core = ctx % 2
    place = ctx // 2
    places = ctx_count // 2
    half = places // 2
    across = group + 1 - 2 * (group % 2)
    other = ctx + 1 - 2 * core
    quarter = (group % 2) * 2 + core
    rank = place // 2 + (place % 2) * (places - 1 - 2 * (place // 2))
    sign = 1 - 2 * core

    tokens = proj.shape[0]
    chans = skip.shape[0] * LANES
    tiles = skip.shape[0]
    poles = pole.shape[0]
    w_rows = w_in.shape[0]
    width = w_in.shape[1] // 4
    cols = width // PHASES
    hops = [1]
    while hops[-1] * 2 < ctx_count:
        hops.append(hops[-1] * 2)

    def place_at(r):
        r = (r + 2 * places) % places
        h = r // half
        return 2 * (r + h * (places - 1 - 2 * r)) + h

    ahead = 2 * place_at(rank + sign) + core
    behind = 2 * place_at(rank - sign) + core

    barrier = pltpu.get_barrier_semaphore()
    greeted = [(group, other), (across, ctx), (across, other), (group, ahead), (group, behind)]
    for hop in hops:
        greeted.append((group, (ctx + hop) % ctx_count))
        greeted.append((group, (ctx + ctx_count - hop) % ctx_count))
    for device in greeted:
        pl.semaphore_signal(barrier, inc=1, device_id=device, device_id_type=MESH)
    pl.semaphore_wait(barrier, len(greeted))

    def remote(src, dst, send, recv, device):
        return pltpu.make_async_remote_copy(
            src_ref=src, dst_ref=dst, send_sem=send, recv_sem=recv,
            device_id=device, device_id_type=MESH,
        )

    pending = []

    def begin(copy):
        copy.start()
        pending.append(copy)
        return copy

    edge = min(16, tokens)
    halo_copy = remote(
        proj.at[pl.ds(tokens - edge, edge)], halo, halo_sem.at[0], halo_sem.at[1],
        (group, (ctx + 1) % ctx_count),
    )

    @pl.when(ctx + 1 < ctx_count)
    def _():
        halo_copy.start()

    my_rows = pl.ds(pl.multiple_of(ctx * w_rows, w_rows), w_rows)
    other_rows = pl.ds(pl.multiple_of(other * w_rows, w_rows), w_rows)
    their_quarter = (group % 2) * 2 + 1 - core

    def part(q, s):
        return pl.ds(pl.multiple_of(q * width + s * cols, cols), cols)

    mate_copies = []
    own_copies = []
    for s in range(PHASES):
        mate_copies.append(begin(remote(
            w_in.at[:, part(their_quarter, s)], w_all.at[s, my_rows],
            mate_sem.at[0, s], mate_sem.at[1, s], (group, other),
        )))
        own = pltpu.make_async_copy(w_in.at[:, part(quarter, s)], w_all.at[s, my_rows], own_sem.at[s])
        own.start()
        own_copies.append(own)

    def ring_copy(d, s, t):
        if d == 0:
            origin = 2 * place_at(rank - sign * t) + core
            device = (group, ahead)
        else:
            origin = 2 * place_at(rank + sign * t) + 1 - core
            device = (group, behind)
        rows = pl.ds(pl.multiple_of(origin * w_rows, w_rows), w_rows)
        dst = w_all.at[s, rows]
        src = w_in.at[:, part(quarter, s)] if d == 0 and t == 0 else dst
        return remote(src, dst, ring_send.at[d, s, t], ring_recv.at[d, s, t], device)

    ring = {}

    def event(s, t):
        for d in range(2):
            if t > 0:
                ring[d, s, t - 1].wait_recv()
            elif d == 1:
                mate_copies[s].wait_recv()
            if t < places - 1:
                ring[d, s, t] = begin(ring_copy(d, s, t))

    events = sorted(
        [(t + SKEW * s, s, t) for s in range(PHASES) for t in range(places)]
    )
    done = [0]

    def run_events(n):
        for _ in range(n):
            if done[0] < len(events):
                _, s, t = events[done[0]]
                event(s, t)
                done[0] += 1

    def phase_over(s):
        return events.index((places - 1 + SKEW * s, s, places - 1)) + 1

    run_events(3)

    def spread(c, carry):
        lanes = pl.ds(pl.multiple_of(c * LANES, LANES), LANES)
        p = pole[:, lanes]
        gain = jnp.sqrt((1.0 - p) * (1.0 + p))
        rows = pl.ds(c, poles, stride=tiles)
        pole_t[rows, :] = p
        coef_t[rows, :] = res[:, lanes] * gain
        left = tokens
        power = p
        total = None
        while left:
            if left & 1:
                total = power if total is None else total * power
            left >>= 1
            if left:
                power = power * power
        decay[rows, :] = total
        return carry

    lax.fori_loop(0, tiles, spread, 0)

    @pl.when(ctx > 0)
    def _():
        halo_copy.wait_recv()

    @pl.when(ctx == 0)
    def _():
        halo[...] = jnp.zeros(halo.shape, halo.dtype)

    row = lax.broadcasted_iota(jnp.int32, (tokens, LANES), 0)

    def smooth(col):
        lanes = pl.ds(pl.multiple_of(col, LANES), LANES)
        x = proj[:, lanes].astype(jnp.float32)
        rim = halo[:, lanes].astype(jnp.float32)
        near = rim[edge - 1 : edge]
        far = rim[edge - 2 : edge - 1]
        back1 = jnp.where(row == 0, near, pltpu.roll(x, 1, 0))
        back2 = jnp.where(row == 0, far, jnp.where(row == 1, near, pltpu.roll(x, 2, 0)))
        return taps[0:1, lanes] * x + taps[1:2, lanes] * back1 + taps[2:3, lanes] * back2

    def make_drive(c, carry):
        drive[pl.ds(c, tokens, stride=tiles), :] = smooth(chans + c * LANES) * smooth(2 * chans + c * LANES)
        return carry

    def make_query(c, carry):
        query[:, pl.ds(pl.multiple_of(c * LANES, LANES), LANES)] = smooth(c * LANES)
        return carry

    pieces = tiles // 8

    def end_state(h):
        p = [pole_t[n * tiles + h * 8 : n * tiles + h * 8 + 8] for n in range(poles)]

        def step(t, state):
            d = drive[pl.ds(pl.multiple_of(t * tiles + h * 8, 8), 8)]
            return tuple(p[n] * state[n] + d for n in range(poles))

        zero = tuple(jnp.zeros((8, LANES), jnp.float32) for _ in range(poles))
        state = lax.fori_loop(0, tokens, step, zero, unroll=4)
        for n in range(poles):
            sent[0, n * tiles + h * 8 : n * tiles + h * 8 + 8] = state[n]

    for h in range(pieces):
        lax.fori_loop(h * 8, h * 8 + 8, make_drive, 0)
        run_events(1)
        end_state(h)
        run_events(1)

    def state_copy(slot, buf, hop):
        return remote(
            sent.at[buf], came.at[slot], state_sem.at[0, slot], state_sem.at[1, slot],
            (group, (ctx + hop) % ctx_count),
        )

    state_copies = []

    def state_start(slot, buf, hop):
        copy = state_copy(slot, buf, hop)
        state_copies.append((copy, hop))

        @pl.when(ctx + hop < ctx_count)
        def _():
            copy.start()

        return copy

    first = state_start(0, 0, 1)
    second = state_start(1, 0, 2)
    run_events(1)
    lax.fori_loop(0, tiles // 2, make_query, 0)
    run_events(1)
    sent[1] = jnp.zeros(sent.shape[1:], jnp.float32)

    @pl.when(ctx >= 1)
    def _():
        first.wait_recv()
        sent[1] = came[0]

    @pl.when(ctx >= 2)
    def _():
        second.wait_recv()
        sent[1] = sent[1] + decay[...] * came[1]

    buf = 1
    for k, hop in enumerate(hops[1:]):
        copy = state_start(2 + k, buf, hop)
        decay[...] = decay[...] * decay[...]
        run_events(1)
        if k == 0:
            lax.fori_loop(tiles // 2, tiles, make_query, 0)
        run_events(1)
        sent[buf + 1] = sent[buf]

        @pl.when(ctx >= hop)
        def _():
            copy.wait_recv()
            sent[buf + 1] = sent[buf] + decay[...] * came[2 + k]

        buf += 1

    def respond(h):
        p = [pole_t[n * tiles + h * 8 : n * tiles + h * 8 + 8] for n in range(poles)]
        q = [coef_t[n * tiles + h * 8 : n * tiles + h * 8 + 8] for n in range(poles)]
        direct = skip[h * 8 : h * 8 + 8]

        def step(t, state):
            at = pl.ds(pl.multiple_of(t * tiles + h * 8, 8), 8)
            d = drive[at]
            state = tuple(p[n] * state[n] + d for n in range(poles))
            terms = [q[n] * state[n] for n in range(poles)] + [direct * d]
            while len(terms) > 1:
                terms = [a + b for a, b in zip(terms[::2], terms[1::2])] + terms[len(terms) & ~1 :]
            filt[at] = terms[0]
            return state

        start = tuple(sent[buf, n * tiles + h * 8 : n * tiles + h * 8 + 8] for n in range(poles))
        lax.fori_loop(0, tokens, step, start, unroll=2)

    def gate(c, carry):
        lanes = pl.ds(pl.multiple_of(c * LANES, LANES), LANES)
        value = query[:, lanes] * filt[pl.ds(c, tokens, stride=tiles), :]
        gated[quarter, :, lanes] = value.astype(jnp.bfloat16)
        return carry

    slot_across = (quarter + 2) % 4
    span = chans // pieces
    direct_copies = []
    for h in range(pieces):
        respond(h)
        lax.fori_loop(h * 8, h * 8 + 8, gate, 0)
        mine = gated.at[quarter, :, h * span : (h + 1) * span]
        direct_copies.append((
            begin(remote(mine, mine, gate_sem.at[0, 0, h], gate_sem.at[1, 0, h], (across, ctx))),
            begin(remote(mine, mine, gate_sem.at[0, 1, h], gate_sem.at[1, 1, h], (group, other))),
        ))
        run_events(2)

    forwards = []
    for h in range(pieces):
        run_events(3)
        direct_copies[h][0].wait_recv()
        theirs = gated.at[slot_across, :, h * span : (h + 1) * span]
        forwards.append(begin(remote(theirs, theirs, fwd_sem.at[0, h], fwd_sem.at[1, h], (group, other))))
    run_events(2)
    for h in range(pieces):
        direct_copies[h][1].wait_recv()
        forwards[h].wait_recv()

    mates = [(group, other), (across, ctx), (across, other)]
    mate_slots = [(group % 2) * 2 + 1 - core, slot_across, (across % 2) * 2 + 1 - core]
    returns = []
    keeps = []
    for s in range(PHASES):
        run_events(phase_over(s) - done[0])
        own_copies[s].wait()

        def block(i, carry):
            left = gated[pl.ds(2 * i, 2)].reshape(2 * tokens, chans)
            value = jnp.dot(left, w_all[s], preferred_element_type=jnp.float32)
            prod[s, pl.ds(2 * i, 2)] = value.astype(jnp.bfloat16).reshape(2, tokens, cols)
            return carry

        lax.fori_loop(0, 2, block, 0)
        where = out.at[:, part(quarter, s)]
        for k in (1, 2, 0):
            returns.append(begin(remote(
                prod.at[s, mate_slots[k]], where, prod_sem.at[0, k, s], prod_sem.at[1, k, s], mates[k],
            )))
        keep = pltpu.make_async_copy(prod.at[s, quarter], where, keep_sem.at[s])
        keep.start()
        keeps.append(keep)

    for copy in returns:
        copy.wait_recv()
    for keep in keeps:
        keep.wait()
    for copy in pending:
        copy.wait_send()

    @pl.when(ctx + 1 < ctx_count)
    def _():
        halo_copy.wait_send()

    for copy, hop in state_copies:

        @pl.when(ctx + hop < ctx_count)
        def _():
            copy.wait_send()


def local(ctx_count, projected, short_filter, modal_pole, residue, skip_weight, out_weight):
    tokens = projected.shape[0]
    chans, poles = modal_pole.shape
    w_rows, width = out_weight.shape
    tiles = chans // LANES
    cols = width // 4 // PHASES
    places = ctx_count // 2
    hop_count = (ctx_count - 1).bit_length()
    dma = pltpu.SemaphoreType.DMA
    whole = pl.BlockSpec(memory_space=pltpu.VMEM)
    anywhere = pl.BlockSpec(memory_space=pl.ANY)
    f32, bf16 = jnp.float32, jnp.bfloat16
    pieces = tiles // 8
    return pl.pallas_call(
        functools.partial(kernel, ctx_count),
        out_shape=jax.ShapeDtypeStruct((tokens, width), bf16),
        in_specs=[whole] * 5 + [anywhere],
        out_specs=anywhere,
        scratch_shapes=[
            pltpu.VMEM((min(16, tokens), 3 * chans), bf16),
            pltpu.VMEM((poles * tiles, LANES), f32),
            pltpu.VMEM((poles * tiles, LANES), f32),
            pltpu.VMEM((poles * tiles, LANES), f32),
            pltpu.VMEM((tokens * tiles, LANES), f32),
            pltpu.VMEM((tokens * tiles, LANES), f32),
            pltpu.VMEM((tokens, chans), f32),
            pltpu.VMEM((hop_count + 1, poles * tiles, LANES), f32),
            pltpu.VMEM((hop_count + 1, poles * tiles, LANES), f32),
            pltpu.VMEM((4, tokens, chans), bf16),
            pltpu.VMEM((PHASES, chans, cols), bf16),
            pltpu.VMEM((PHASES, 4, tokens, cols), bf16),
            dma((2,)),
            dma((2, PHASES)),
            dma((PHASES,)),
            dma((2, PHASES, places - 1)),
            dma((2, PHASES, places - 1)),
            dma((2, hop_count + 1)),
            dma((2, 2, pieces)),
            dma((2, pieces)),
            dma((2, 3, PHASES)),
            dma((PHASES,)),
        ],
        compiler_params=pltpu.CompilerParams(
            collective_id=0, has_side_effects=True, vmem_limit_bytes=40 * 1024 * 1024
        ),
    )(
        projected, short_filter, modal_pole.T, residue.T,
        skip_weight.reshape(tiles, LANES), out_weight,
    )


def solution(mesh):
    placed = (P(("groups", "ctx"), None), P(), P(), P(), P(), P("ctx", None))
    return jax.shard_map(
        functools.partial(local, mesh.shape["ctx"]), mesh=mesh, in_specs=placed,
        out_specs=P(("groups", "ctx"), None), check_vma=False,
    )
```

```python
import functools

import jax
import jax.numpy as jnp
from jax import lax
from jax.experimental import pallas as pl
from jax.experimental.pallas import tpu as pltpu
from jax.sharding import PartitionSpec as P

MESH = pl.DeviceIdType.MESH
LANES = 128
PHASES = 4
LEVEL = 4
PART = 4
SKEW = 0
PACE = (4, 1, 1, 1, 2, 2, 1, 1, 2, 2)


def kernel(
    ctx_count, proj_in, taps_in, pole_in, res_in, skip_in, w_in, out,
    proj, taps, pole, res, skip,
    halo, pole_t, coef_t, decay, drive, filt, query, sent, came, starts, origin, gated, w_all, prod,
    load_sem, halo_sem, mate_sem, own_sem, ring_send, ring_recv, state_sem, start_sem, gate_sem, fwd_sem, prod_sem, keep_sem,
):
    group = lax.axis_index("groups")
    ctx = lax.axis_index("ctx")
    core = ctx % 2
    place = ctx // 2
    places = ctx_count // 2
    half = places // 2
    across = group + 1 - 2 * (group % 2)
    other = ctx + 1 - 2 * core
    quarter = (group % 2) * 2 + core
    rank = place // 2 + (place % 2) * (places - 1 - 2 * (place // 2))
    sign = 1 - 2 * core

    tokens = proj.shape[0]
    chans = skip.shape[0] * LANES
    tiles = skip.shape[0]
    poles = pole.shape[0]
    w_rows = w_in.shape[0]
    width = w_in.shape[1] // 4
    cols = width // PHASES
    workers = min(ctx_count, poles * tiles // 8)
    share = poles * tiles // workers

    def place_at(r):
        r = (r + 2 * places) % places
        h = r // half
        return 2 * (r + h * (places - 1 - 2 * r)) + h

    ahead = 2 * place_at(rank + sign) + core
    behind = 2 * place_at(rank - sign) + core

    barrier = pltpu.get_barrier_semaphore()
    greeted = [(across, ctx), (across, other)]
    for step in range(1, ctx_count):
        greeted.append((group, (ctx + step) % ctx_count))
    for device in greeted:
        pl.semaphore_signal(barrier, inc=1, device_id=device, device_id_type=MESH)
    loads = []
    for k, (src, dst) in enumerate(
        ((pole_in, pole), (res_in, res), (skip_in, skip), (taps_in, taps), (proj_in, proj))
    ):
        loads.append(pltpu.make_async_copy(src, dst, load_sem.at[k]))
        loads[-1].start()
    pl.semaphore_wait(barrier, len(greeted))

    def remote(src, dst, send, recv, device):
        return pltpu.make_async_remote_copy(
            src_ref=src, dst_ref=dst, send_sem=send, recv_sem=recv,
            device_id=device, device_id_type=MESH,
        )

    pending = []

    def begin(copy):
        copy.start()
        pending.append(copy)
        return copy

    edge = min(16, tokens)
    halo_copy = remote(
        proj_in.at[pl.ds(tokens - edge, edge)], halo, halo_sem.at[0], halo_sem.at[1],
        (group, (ctx + 1) % ctx_count),
    )

    @pl.when(ctx + 1 < ctx_count)
    def _():
        halo_copy.start()

    my_rows = pl.ds(pl.multiple_of(ctx * w_rows, w_rows), w_rows)
    other_rows = pl.ds(pl.multiple_of(other * w_rows, w_rows), w_rows)
    their_quarter = (group % 2) * 2 + 1 - core

    def part(q, s):
        return pl.ds(pl.multiple_of(q * width + s * cols, cols), cols)

    def ring_copy(d, s, t):
        if d == 0:
            origin = 2 * place_at(rank - sign * t) + core
            device = (group, ahead)
        else:
            origin = 2 * place_at(rank + sign * t) + 1 - core
            device = (group, behind)
        rows = pl.ds(pl.multiple_of(origin * w_rows, w_rows), w_rows)
        dst = w_all.at[s, rows]
        src = w_in.at[:, part(quarter, s)] if d == 0 and t == 0 else dst
        return remote(src, dst, ring_send.at[d, s, t], ring_recv.at[d, s, t], device)

    ring = {}
    mate_copies = []
    own_copies = []
    for s in range(PHASES):
        ring[0, s, 0] = begin(ring_copy(0, s, 0))
        mate_copies.append(begin(remote(
            w_in.at[:, part(their_quarter, s)], w_all.at[s, my_rows],
            mate_sem.at[0, s], mate_sem.at[1, s], (group, other),
        )))
        own = pltpu.make_async_copy(w_in.at[:, part(quarter, s)], w_all.at[s, my_rows], own_sem.at[s])
        own_copies.append(own)
    for own in own_copies:
        own.start()


    def event(s, t):
        for d in range(2):
            if t == 0 and d == 0:
                continue
            if t > 0:
                ring[d, s, t - 1].wait_recv()
            else:
                mate_copies[s].wait_recv()
            if t < places - 1:
                ring[d, s, t] = begin(ring_copy(d, s, t))

    def order(s, t):
        return t + (SKEW * (s // 2) if t > LEVEL else 0)

    events = sorted([(order(s, t), s, t) for s in range(PHASES) for t in range(places)])
    done = [0]

    def run_events(n):
        for _ in range(n):
            if done[0] < len(events):
                _, s, t = events[done[0]]
                event(s, t)
                done[0] += 1

    def phase_over(s):
        return events.index((order(s, places - 1), s, places - 1)) + 1

    for load in loads:
        load.wait()

    def spread(c, carry):
        lanes = pl.ds(pl.multiple_of(c * LANES, LANES), LANES)
        p = pole[:, lanes]
        gain = jnp.sqrt((1.0 - p) * (1.0 + p))
        rows = pl.ds(c, poles, stride=tiles)
        pole_t[rows, :] = p
        coef_t[rows, :] = res[:, lanes] * gain
        left = tokens
        power = p
        total = None
        while left:
            if left & 1:
                total = power if total is None else total * power
            left >>= 1
            if left:
                power = power * power
        decay[rows, :] = total
        return carry

    lax.fori_loop(0, tiles, spread, 0)

    run_events(PACE[0])

    @pl.when(ctx > 0)
    def _():
        halo_copy.wait_recv()

    @pl.when(ctx == 0)
    def _():
        halo[...] = jnp.zeros(halo.shape, halo.dtype)

    row = lax.broadcasted_iota(jnp.int32, (tokens, LANES), 0)

    def smooth(col):
        lanes = pl.ds(pl.multiple_of(col, LANES), LANES)
        x = proj[:, lanes].astype(jnp.float32)
        rim = halo[:, lanes].astype(jnp.float32)
        near = rim[edge - 1 : edge]
        far = rim[edge - 2 : edge - 1]
        back1 = jnp.where(row == 0, near, pltpu.roll(x, 1, 0))
        back2 = jnp.where(row == 0, far, jnp.where(row == 1, near, pltpu.roll(x, 2, 0)))
        return taps[0:1, lanes] * x + taps[1:2, lanes] * back1 + taps[2:3, lanes] * back2

    def make_drive(c, carry):
        drive[pl.ds(c, tokens, stride=tiles), :] = smooth(chans + c * LANES) * smooth(2 * chans + c * LANES)
        return carry

    def make_query(c, carry):
        query[:, pl.ds(pl.multiple_of(c * LANES, LANES), LANES)] = smooth(c * LANES)
        return carry

    pieces = tiles // 8

    def end_state(h):
        p = [pole_t[n * tiles + h * 8 : n * tiles + h * 8 + 8] for n in range(poles)]

        def step(t, state):
            d = drive[pl.ds(pl.multiple_of(t * tiles + h * 8, 8), 8)]
            return tuple(p[n] * state[n] + d for n in range(poles))

        zero = tuple(jnp.zeros((8, LANES), jnp.float32) for _ in range(poles))
        state = lax.fori_loop(0, tokens, step, zero, unroll=4)
        for n in range(poles):
            sent[n * tiles + h * 8 : n * tiles + h * 8 + 8] = state[n]

    for h in range(pieces):
        lax.fori_loop(h * 8, h * 8 + 8, make_drive, 0)
        run_events(PACE[2])
        end_state(h)
        run_events(PACE[3])

    def rows_of(index):
        return pl.ds(pl.multiple_of(index * share, share), share)

    def if_worker(index, body):
        if workers == ctx_count:
            body()
        else:
            pl.when(index < workers)(body)

    at_step = [(ctx + step) % ctx_count for step in range(ctx_count)]
    ends = [None]
    begins = [None]
    for step in range(1, ctx_count):
        ends.append(remote(
            sent.at[rows_of(at_step[step] % workers)], came.at[step],
            state_sem.at[0, step], state_sem.at[1, step], (group, at_step[step]),
        ))
        begins.append(remote(
            starts.at[at_step[step]], origin.at[rows_of(ctx % workers)],
            start_sem.at[0, step], start_sem.at[1, step], (group, at_step[step]),
        ))
    for step in range(1, ctx_count):
        if_worker(at_step[step], ends[step].start)
    lax.fori_loop(0, tiles, make_query, 0)
    run_events(PACE[4])

    def combine():
        mine = rows_of(ctx % workers)
        came[0] = sent[mine]
        for step in range(1, ctx_count):
            ends[step].wait_recv()
        fade = decay[mine]

        def add(j, state):
            starts[j] = state
            return fade * state + came[(ctx + ctx_count - j) % ctx_count]

        lax.fori_loop(0, ctx_count, add, jnp.zeros((share, LANES), jnp.float32))
        origin[mine] = starts[ctx]
        for step in range(1, ctx_count):
            begins[step].start()

    if_worker(ctx, combine)
    run_events(PACE[5])
    for step in range(1, ctx_count):
        if_worker((ctx + ctx_count - step) % ctx_count, begins[step].wait_recv)

    def respond(h):
        p = [pole_t[n * tiles + h * 8 : n * tiles + h * 8 + 8] for n in range(poles)]
        q = [coef_t[n * tiles + h * 8 : n * tiles + h * 8 + 8] for n in range(poles)]
        direct = skip[h * 8 : h * 8 + 8]

        def step(t, state):
            at = pl.ds(pl.multiple_of(t * tiles + h * 8, 8), 8)
            d = drive[at]
            state = tuple(p[n] * state[n] + d for n in range(poles))
            terms = [q[n] * state[n] for n in range(poles)] + [direct * d]
            while len(terms) > 1:
                terms = [a + b for a, b in zip(terms[::2], terms[1::2])] + terms[len(terms) & ~1 :]
            filt[at] = terms[0]
            return state

        start = tuple(origin[n * tiles + h * 8 : n * tiles + h * 8 + 8] for n in range(poles))
        lax.fori_loop(0, tokens, step, start, unroll=2)

    def gate(c, carry):
        lanes = pl.ds(pl.multiple_of(c * LANES, LANES), LANES)
        value = query[:, lanes] * filt[pl.ds(c, tokens, stride=tiles), :]
        gated[quarter, :, lanes] = value.astype(jnp.bfloat16)
        return carry

    slot_across = (quarter + 2) % 4
    parts = tiles // PART
    span = PART * LANES
    direct_copies = []
    for h in range(pieces):
        respond(h)
        for u in range(h * 8 // PART, (h + 1) * 8 // PART):
            lax.fori_loop(u * PART, (u + 1) * PART, gate, 0)
            mine = gated.at[quarter, :, u * span : (u + 1) * span]
            direct_copies.append((
                begin(remote(mine, mine, gate_sem.at[0, 0, u], gate_sem.at[1, 0, u], (across, ctx))),
                begin(remote(mine, mine, gate_sem.at[0, 1, u], gate_sem.at[1, 1, u], (group, other))),
            ))
        run_events(PACE[6 + h % 2])

    forwards = []
    for u in range(parts):
        run_events(PACE[8])
        direct_copies[u][0].wait_recv()
        theirs = gated.at[slot_across, :, u * span : (u + 1) * span]
        forwards.append(begin(remote(theirs, theirs, fwd_sem.at[0, u], fwd_sem.at[1, u], (group, other))))
    run_events(PACE[9])
    for u in range(parts):
        direct_copies[u][1].wait_recv()
        forwards[u].wait_recv()

    mates = [(group, other), (across, ctx), (across, other)]
    mate_slots = [(group % 2) * 2 + 1 - core, slot_across, (across % 2) * 2 + 1 - core]
    returns = []
    keeps = []
    for s in range(PHASES):
        run_events(phase_over(s) - done[0])
        own_copies[s].wait()

        def block(i, carry):
            left = gated[pl.ds(2 * i, 2)].reshape(2 * tokens, chans)
            value = jnp.dot(left, w_all[s], preferred_element_type=jnp.float32)
            prod[s, pl.ds(2 * i, 2)] = value.astype(jnp.bfloat16).reshape(2, tokens, cols)
            return carry

        lax.fori_loop(0, 2, block, 0)
        where = out.at[:, part(quarter, s)]
        for k in (1, 2, 0):
            returns.append(begin(remote(
                prod.at[s, mate_slots[k]], where, prod_sem.at[0, k, s], prod_sem.at[1, k, s], mates[k],
            )))
        keep = pltpu.make_async_copy(prod.at[s, quarter], where, keep_sem.at[s])
        keep.start()
        keeps.append(keep)

    for copy in returns:
        copy.wait_recv()
    for keep in keeps:
        keep.wait()
    for copy in pending:
        copy.wait_send()

    @pl.when(ctx + 1 < ctx_count)
    def _():
        halo_copy.wait_send()

    for step in range(1, ctx_count):
        if_worker(at_step[step], ends[step].wait_send)
        if_worker(ctx, begins[step].wait_send)


def local(ctx_count, projected, short_filter, modal_pole, residue, skip_weight, out_weight):
    tokens = projected.shape[0]
    chans, poles = modal_pole.shape
    w_rows, width = out_weight.shape
    tiles = chans // LANES
    cols = width // 4 // PHASES
    places = ctx_count // 2
    workers = min(ctx_count, poles * tiles // 8)
    share = poles * tiles // workers
    dma = pltpu.SemaphoreType.DMA
    hbm = pl.BlockSpec(memory_space=pltpu.HBM)
    f32, bf16 = jnp.float32, jnp.bfloat16
    return pl.pallas_call(
        functools.partial(kernel, ctx_count),
        out_shape=jax.ShapeDtypeStruct((tokens, width), bf16),
        in_specs=[hbm] * 6,
        out_specs=hbm,
        scratch_shapes=[
            pltpu.VMEM((tokens, 3 * chans), bf16),
            pltpu.VMEM(short_filter.shape, f32),
            pltpu.VMEM((poles, chans), f32),
            pltpu.VMEM((poles, chans), f32),
            pltpu.VMEM((tiles, LANES), f32),
            pltpu.VMEM((min(16, tokens), 3 * chans), bf16),
            pltpu.VMEM((poles * tiles, LANES), f32),
            pltpu.VMEM((poles * tiles, LANES), f32),
            pltpu.VMEM((poles * tiles, LANES), f32),
            pltpu.VMEM((tokens * tiles, LANES), f32),
            pltpu.VMEM((tokens * tiles, LANES), f32),
            pltpu.VMEM((tokens, chans), f32),
            pltpu.VMEM((poles * tiles, LANES), f32),
            pltpu.VMEM((ctx_count, share, LANES), f32),
            pltpu.VMEM((ctx_count, share, LANES), f32),
            pltpu.VMEM((poles * tiles, LANES), f32),
            pltpu.VMEM((4, tokens, chans), bf16),
            pltpu.VMEM((PHASES, chans, cols), bf16),
            pltpu.VMEM((PHASES, 4, tokens, cols), bf16),
            dma((5,)),
            dma((2,)),
            dma((2, PHASES)),
            dma((PHASES,)),
            dma((2, PHASES, places - 1)),
            dma((2, PHASES, places - 1)),
            dma((2, ctx_count)),
            dma((2, ctx_count)),
            dma((2, 2, tiles // PART)),
            dma((2, tiles // PART)),
            dma((2, 3, PHASES)),
            dma((PHASES,)),
        ],
        compiler_params=pltpu.CompilerParams(
            collective_id=0, has_side_effects=True, vmem_limit_bytes=63 * 1024 * 1024
        ),
    )(
        projected, short_filter, modal_pole.T, residue.T,
        skip_weight.reshape(tiles, LANES), out_weight,
    )


def solution(mesh):
    placed = (P(("groups", "ctx"), None), P(), P(), P(), P(), P("ctx", None))
    return jax.shard_map(
        functools.partial(local, mesh.shape["ctx"]), mesh=mesh, in_specs=placed,
        out_specs=P(("groups", "ctx"), None), check_vma=False,
    )
```

```python
import functools

import jax
import jax.numpy as jnp
from jax import lax
from jax.experimental import pallas as pl
from jax.experimental.pallas import tpu as pltpu
from jax.sharding import PartitionSpec as P

MESH = pl.DeviceIdType.MESH
LANES = 128
PHASES = 4
LEVEL = 4
PART = 4
SKEW = 0
PACE = (4, 1, 2, 1, 3, 3, 2, 2, 2, 2)


def kernel(
    ctx_count, proj_in, taps_in, pole_in, res_in, skip_in, w_in, out,
    proj, taps, pole, res, skip,
    halo, pole_t, coef_t, decay, drive, filt, query, sent, came, starts, origin, gated, w_all, prod,
    load_sem, halo_sem, mate_sem, own_sem, ring_send, ring_recv, state_sem, start_sem, gate_sem, fwd_sem, prod_sem, keep_sem,
):
    group = lax.axis_index("groups")
    ctx = lax.axis_index("ctx")
    core = ctx % 2
    place = ctx // 2
    places = ctx_count // 2
    half = places // 2
    across = group + 1 - 2 * (group % 2)
    other = ctx + 1 - 2 * core
    quarter = (group % 2) * 2 + core
    rank = place // 2 + (place % 2) * (places - 1 - 2 * (place // 2))
    sign = 1 - 2 * core

    tokens = proj.shape[0]
    chans = skip.shape[0] * LANES
    tiles = skip.shape[0]
    poles = pole.shape[0]
    w_rows = w_in.shape[0]
    width = w_in.shape[1] // 4
    cols = width // PHASES
    workers = min(ctx_count, poles * tiles // 8)
    share = poles * tiles // workers

    def place_at(r):
        r = (r + 2 * places) % places
        h = r // half
        return 2 * (r + h * (places - 1 - 2 * r)) + h

    ahead = 2 * place_at(rank + sign) + core
    behind = 2 * place_at(rank - sign) + core

    barrier = pltpu.get_barrier_semaphore()
    greeted = [(across, ctx), (across, other)]
    for step in range(1, ctx_count):
        greeted.append((group, (ctx + step) % ctx_count))
    for device in greeted:
        pl.semaphore_signal(barrier, inc=1, device_id=device, device_id_type=MESH)
    loads = []
    for k, (src, dst) in enumerate(
        ((pole_in, pole), (res_in, res), (skip_in, skip), (taps_in, taps), (proj_in, proj))
    ):
        loads.append(pltpu.make_async_copy(src, dst, load_sem.at[k]))
        loads[-1].start()
    pl.semaphore_wait(barrier, len(greeted))

    def remote(src, dst, send, recv, device):
        return pltpu.make_async_remote_copy(
            src_ref=src, dst_ref=dst, send_sem=send, recv_sem=recv,
            device_id=device, device_id_type=MESH,
        )

    pending = []

    def begin(copy):
        copy.start()
        pending.append(copy)
        return copy

    edge = min(16, tokens)
    halo_copy = remote(
        proj_in.at[pl.ds(tokens - edge, edge)], halo, halo_sem.at[0], halo_sem.at[1],
        (group, (ctx + 1) % ctx_count),
    )

    @pl.when(ctx + 1 < ctx_count)
    def _():
        halo_copy.start()

    my_rows = pl.ds(pl.multiple_of(ctx * w_rows, w_rows), w_rows)
    other_rows = pl.ds(pl.multiple_of(other * w_rows, w_rows), w_rows)
    their_quarter = (group % 2) * 2 + 1 - core

    def part(q, s):
        return pl.ds(pl.multiple_of(q * width + s * cols, cols), cols)

    def ring_copy(d, s, t):
        if d == 0:
            origin = 2 * place_at(rank - sign * t) + core
            device = (group, ahead)
        else:
            origin = 2 * place_at(rank + sign * t) + 1 - core
            device = (group, behind)
        rows = pl.ds(pl.multiple_of(origin * w_rows, w_rows), w_rows)
        dst = w_all.at[s, rows]
        src = w_in.at[:, part(quarter, s)] if d == 0 and t == 0 else dst
        return remote(src, dst, ring_send.at[d, s, t], ring_recv.at[d, s, t], device)

    ring = {}
    mate_copies = []
    own_copies = []
    for s in range(PHASES):
        mate_copies.append(begin(remote(
            w_in.at[:, part(their_quarter, s)], w_all.at[s, my_rows],
            mate_sem.at[0, s], mate_sem.at[1, s], (group, other),
        )))
        own = pltpu.make_async_copy(w_in.at[:, part(quarter, s)], w_all.at[s, my_rows], own_sem.at[s])
        own_copies.append(own)
    for s in range(PHASES):
        ring[0, s, 0] = begin(ring_copy(0, s, 0))
    for own in own_copies:
        own.start()


    def event(s, t):
        for d in range(2):
            if t == 0 and d == 0:
                continue
            if t > 0:
                ring[d, s, t - 1].wait_recv()
            else:
                mate_copies[s].wait_recv()
            if t < places - 1:
                ring[d, s, t] = begin(ring_copy(d, s, t))

    def order(s, t):
        return t + (SKEW * (s // 2) if t > LEVEL else 0)

    events = sorted([(order(s, t), s, t) for s in range(PHASES) for t in range(places)])
    done = [0]

    def run_events(n):
        for _ in range(n):
            if done[0] < len(events):
                _, s, t = events[done[0]]
                event(s, t)
                done[0] += 1

    def phase_over(s):
        return events.index((order(s, places - 1), s, places - 1)) + 1

    for load in loads:
        load.wait()

    def spread(c, carry):
        lanes = pl.ds(pl.multiple_of(c * LANES, LANES), LANES)
        p = pole[:, lanes]
        gain = jnp.sqrt((1.0 - p) * (1.0 + p))
        rows = pl.ds(c, poles, stride=tiles)
        pole_t[rows, :] = p
        coef_t[rows, :] = res[:, lanes] * gain
        left = tokens
        power = p
        total = None
        while left:
            if left & 1:
                total = power if total is None else total * power
            left >>= 1
            if left:
                power = power * power
        decay[rows, :] = total
        return carry

    lax.fori_loop(0, tiles, spread, 0)

    run_events(PACE[0])

    @pl.when(ctx > 0)
    def _():
        halo_copy.wait_recv()

    @pl.when(ctx == 0)
    def _():
        halo[...] = jnp.zeros(halo.shape, halo.dtype)

    row = lax.broadcasted_iota(jnp.int32, (tokens, LANES), 0)

    def smooth(col):
        lanes = pl.ds(pl.multiple_of(col, LANES), LANES)
        x = proj[:, lanes].astype(jnp.float32)
        rim = halo[:, lanes].astype(jnp.float32)
        near = rim[edge - 1 : edge]
        far = rim[edge - 2 : edge - 1]
        back1 = jnp.where(row == 0, near, pltpu.roll(x, 1, 0))
        back2 = jnp.where(row == 0, far, jnp.where(row == 1, near, pltpu.roll(x, 2, 0)))
        return taps[0:1, lanes] * x + taps[1:2, lanes] * back1 + taps[2:3, lanes] * back2

    def make_drive(c, carry):
        drive[pl.ds(c, tokens, stride=tiles), :] = smooth(chans + c * LANES) * smooth(2 * chans + c * LANES)
        return carry

    def make_query(c, carry):
        query[:, pl.ds(pl.multiple_of(c * LANES, LANES), LANES)] = smooth(c * LANES)
        return carry

    pieces = tiles // 8

    def end_state(h):
        p = [pole_t[n * tiles + h * 8 : n * tiles + h * 8 + 8] for n in range(poles)]

        def step(t, state):
            d = drive[pl.ds(pl.multiple_of(t * tiles + h * 8, 8), 8)]
            return tuple(p[n] * state[n] + d for n in range(poles))

        zero = tuple(jnp.zeros((8, LANES), jnp.float32) for _ in range(poles))
        state = lax.fori_loop(0, tokens, step, zero, unroll=4)
        for n in range(poles):
            sent[n * tiles + h * 8 : n * tiles + h * 8 + 8] = state[n]

    for h in range(pieces):
        lax.fori_loop(h * 8, h * 8 + 8, make_drive, 0)
        run_events(PACE[2])
        end_state(h)
        run_events(PACE[3])

    def rows_of(index):
        return pl.ds(pl.multiple_of(index * share, share), share)

    def if_worker(index, body):
        if workers == ctx_count:
            body()
        else:
            pl.when(index < workers)(body)

    at_step = [(ctx + step) % ctx_count for step in range(ctx_count)]
    ends = [None]
    begins = [None]
    for step in range(1, ctx_count):
        ends.append(remote(
            sent.at[rows_of(at_step[step] % workers)], came.at[step],
            state_sem.at[0, step], state_sem.at[1, step], (group, at_step[step]),
        ))
        begins.append(remote(
            starts.at[at_step[step]], origin.at[rows_of(ctx % workers)],
            start_sem.at[0, step], start_sem.at[1, step], (group, at_step[step]),
        ))
    for step in range(1, ctx_count):
        if_worker(at_step[step], ends[step].start)
    lax.fori_loop(0, tiles, make_query, 0)
    run_events(PACE[4])

    def combine():
        mine = rows_of(ctx % workers)
        came[0] = sent[mine]
        for step in range(1, ctx_count):
            ends[step].wait_recv()
        fade = decay[mine]

        def add(j, state):
            starts[j] = state
            return fade * state + came[(ctx + ctx_count - j) % ctx_count]

        lax.fori_loop(0, ctx_count, add, jnp.zeros((share, LANES), jnp.float32))
        origin[mine] = starts[ctx]
        for step in range(1, ctx_count):
            begins[step].start()

    if_worker(ctx, combine)
    run_events(PACE[5])
    for step in range(1, ctx_count):
        if_worker((ctx + ctx_count - step) % ctx_count, begins[step].wait_recv)

    def respond(h):
        p = [pole_t[n * tiles + h * 8 : n * tiles + h * 8 + 8] for n in range(poles)]
        q = [coef_t[n * tiles + h * 8 : n * tiles + h * 8 + 8] for n in range(poles)]
        direct = skip[h * 8 : h * 8 + 8]

        def step(t, state):
            at = pl.ds(pl.multiple_of(t * tiles + h * 8, 8), 8)
            d = drive[at]
            state = tuple(p[n] * state[n] + d for n in range(poles))
            terms = [q[n] * state[n] for n in range(poles)] + [direct * d]
            while len(terms) > 1:
                terms = [a + b for a, b in zip(terms[::2], terms[1::2])] + terms[len(terms) & ~1 :]
            filt[at] = terms[0]
            return state

        start = tuple(origin[n * tiles + h * 8 : n * tiles + h * 8 + 8] for n in range(poles))
        lax.fori_loop(0, tokens, step, start, unroll=2)

    def gate(c, carry):
        lanes = pl.ds(pl.multiple_of(c * LANES, LANES), LANES)
        value = query[:, lanes] * filt[pl.ds(c, tokens, stride=tiles), :]
        gated[quarter, :, lanes] = value.astype(jnp.bfloat16)
        return carry

    slot_across = (quarter + 2) % 4
    parts = tiles // PART
    span = PART * LANES
    direct_copies = []
    for h in range(pieces):
        respond(h)
        for u in range(h * 8 // PART, (h + 1) * 8 // PART):
            lax.fori_loop(u * PART, (u + 1) * PART, gate, 0)
            mine = gated.at[quarter, :, u * span : (u + 1) * span]
            direct_copies.append((
                begin(remote(mine, mine, gate_sem.at[0, 0, u], gate_sem.at[1, 0, u], (across, ctx))),
                begin(remote(mine, mine, gate_sem.at[0, 1, u], gate_sem.at[1, 1, u], (group, other))),
            ))
        run_events(PACE[6 + h % 2])

    forwards = []
    for u in range(parts):
        run_events(PACE[8])
        direct_copies[u][0].wait_recv()
        theirs = gated.at[slot_across, :, u * span : (u + 1) * span]
        forwards.append(begin(remote(theirs, theirs, fwd_sem.at[0, u], fwd_sem.at[1, u], (group, other))))
    run_events(PACE[9])
    for u in range(parts):
        direct_copies[u][1].wait_recv()
        forwards[u].wait_recv()

    mates = [(group, other), (across, ctx), (across, other)]
    mate_slots = [(group % 2) * 2 + 1 - core, slot_across, (across % 2) * 2 + 1 - core]
    returns = []
    keeps = []
    for s in range(PHASES):
        run_events(phase_over(s) - done[0])
        own_copies[s].wait()

        def block(i, carry):
            left = gated[pl.ds(2 * i, 2)].reshape(2 * tokens, chans)
            value = jnp.dot(left, w_all[s], preferred_element_type=jnp.float32)
            prod[s, pl.ds(2 * i, 2)] = value.astype(jnp.bfloat16).reshape(2, tokens, cols)
            return carry

        lax.fori_loop(0, 2, block, 0)
        where = out.at[:, part(quarter, s)]
        for k in (1, 2, 0):
            returns.append(begin(remote(
                prod.at[s, mate_slots[k]], where, prod_sem.at[0, k, s], prod_sem.at[1, k, s], mates[k],
            )))
        keep = pltpu.make_async_copy(prod.at[s, quarter], where, keep_sem.at[s])
        keep.start()
        keeps.append(keep)

    for copy in returns:
        copy.wait_recv()
    for keep in keeps:
        keep.wait()
    for copy in pending:
        copy.wait_send()

    @pl.when(ctx + 1 < ctx_count)
    def _():
        halo_copy.wait_send()

    for step in range(1, ctx_count):
        if_worker(at_step[step], ends[step].wait_send)
        if_worker(ctx, begins[step].wait_send)


def local(ctx_count, projected, short_filter, modal_pole, residue, skip_weight, out_weight):
    tokens = projected.shape[0]
    chans, poles = modal_pole.shape
    w_rows, width = out_weight.shape
    tiles = chans // LANES
    cols = width // 4 // PHASES
    places = ctx_count // 2
    workers = min(ctx_count, poles * tiles // 8)
    share = poles * tiles // workers
    dma = pltpu.SemaphoreType.DMA
    hbm = pl.BlockSpec(memory_space=pltpu.HBM)
    f32, bf16 = jnp.float32, jnp.bfloat16
    return pl.pallas_call(
        functools.partial(kernel, ctx_count),
        out_shape=jax.ShapeDtypeStruct((tokens, width), bf16),
        in_specs=[hbm] * 6,
        out_specs=hbm,
        scratch_shapes=[
            pltpu.VMEM((tokens, 3 * chans), bf16),
            pltpu.VMEM(short_filter.shape, f32),
            pltpu.VMEM((poles, chans), f32),
            pltpu.VMEM((poles, chans), f32),
            pltpu.VMEM((tiles, LANES), f32),
            pltpu.VMEM((min(16, tokens), 3 * chans), bf16),
            pltpu.VMEM((poles * tiles, LANES), f32),
            pltpu.VMEM((poles * tiles, LANES), f32),
            pltpu.VMEM((poles * tiles, LANES), f32),
            pltpu.VMEM((tokens * tiles, LANES), f32),
            pltpu.VMEM((tokens * tiles, LANES), f32),
            pltpu.VMEM((tokens, chans), f32),
            pltpu.VMEM((poles * tiles, LANES), f32),
            pltpu.VMEM((ctx_count, share, LANES), f32),
            pltpu.VMEM((ctx_count, share, LANES), f32),
            pltpu.VMEM((poles * tiles, LANES), f32),
            pltpu.VMEM((4, tokens, chans), bf16),
            pltpu.VMEM((PHASES, chans, cols), bf16),
            pltpu.VMEM((PHASES, 4, tokens, cols), bf16),
            dma((5,)),
            dma((2,)),
            dma((2, PHASES)),
            dma((PHASES,)),
            dma((2, PHASES, places - 1)),
            dma((2, PHASES, places - 1)),
            dma((2, ctx_count)),
            dma((2, ctx_count)),
            dma((2, 2, tiles // PART)),
            dma((2, tiles // PART)),
            dma((2, 3, PHASES)),
            dma((PHASES,)),
        ],
        compiler_params=pltpu.CompilerParams(
            collective_id=0, has_side_effects=True, vmem_limit_bytes=63 * 1024 * 1024
        ),
    )(
        projected, short_filter, modal_pole.T, residue.T,
        skip_weight.reshape(tiles, LANES), out_weight,
    )


def solution(mesh):
    placed = (P(("groups", "ctx"), None), P(), P(), P(), P(), P("ctx", None))
    return jax.shard_map(
        functools.partial(local, mesh.shape["ctx"]), mesh=mesh, in_specs=placed,
        out_specs=P(("groups", "ctx"), None), check_vma=False,
    )
```
